32 devices in a mesh: blk: 8 (over z, x), lab: 4 (over y, core).
Axes of the slice: x: 2, y: 2, z: 4, core: 2. Of those that a mesh axis runs over, the one named last changes fastest.
Arguments:
- features: bfloat16 [4096, 768], P(('blk', 'lab')), may hold values from -0.21875 to 0.21875
- direction: bfloat16 [4, 128, 768], P('lab', 'blk'), may hold values from -6 to 6
- active: int32 [4096, 512], P('blk', 'lab'), may hold values 0 or 1
- shortlist: int32 [32, 4], P('blk', 'lab'), may hold values 0 or 1
Outputs:
- hess_product: float32 [4, 128, 768], P('lab', 'blk')
- curvature: float32 [4, 128], P('lab', 'blk')
The draws below stay inside these ranges and needn't reach their ends.
All inputs are finite; a program needn't handle non-finite values. No bound on the sum of `active` or of `shortlist` on one device may be relied on, other than what follows from the above.
Results may differ from the reference program's by a relative error of at most 0.00059.
Values may be sent and summed in bfloat16 or wider, within the bound.
A program may use at most 64 MiB of HBM per device.

```python
import jax
import jax.numpy as jnp
from jax import lax

D = 768
TILE = 128
ROWS = 4096
LGROUP = 128
LABELS = 512
N_LAB = 4


def with_ends(values, key, least, top_value):
    shape = values.shape
    index_at = [jax.random.randint(jax.random.fold_in(key, axis), (), 0, shape[axis]) for axis in range(len(shape))]
    values = values.at[tuple(index_at)].set(least)
    longest = shape.index(max(shape))
    index_at[longest] = (index_at[longest] + 1) % shape[longest]
    return values.at[tuple(index_at)].set(top_value)


def shard_levels(rng, shape, cuts, smallest, top_value):
    level, own = 1.0, jax.random.fold_in(rng, 6)
    for axis_at, parts in cuts:
        draws = jnp.exp(jax.random.uniform(jax.random.fold_in(own, axis_at), (parts,), jnp.float32, smallest / len(cuts), top_value / len(cuts)))
        level = level * jnp.repeat(draws, shape[axis_at] // parts).reshape([-1 if axis == axis_at else 1 for axis in range(len(shape))])
    return level


def scatter_about(own_key, dims, deviation, most, pieces=(), held_as=jnp.bfloat16):
    result = deviation * jax.random.normal(own_key, dims, jnp.float32)
    if pieces:
        result = result * shard_levels(own_key, dims, pieces, -0.22, 0.18)
    return jnp.clip(result, -most, most).astype(held_as)


def setup_inputs(seed: int = 0) -> dict:
    key_list = jax.random.split(jax.random.key(seed), 5)
    features = scatter_about(key_list[0], (ROWS, D), (D ** -0.5), 0.21875, ((0, 32),))
    direction = scatter_about(key_list[1], (N_LAB, LGROUP, D), 1.0, 6.0, ((0, 4), (1, 8)))
    active = with_ends((jax.random.randint(key_list[2], (ROWS, LABELS), 0, 3) < 1).astype(jnp.int32), jax.random.fold_in(key_list[2], 1), 0, 1)
    shortlist = with_ends((jax.random.randint(key_list[3], (ROWS // TILE, LABELS // TILE), 0, 4) < 3).astype(jnp.int32), jax.random.fold_in(key_list[3], 1), 0, 1)
    return dict(features=features, direction=direction, active=active, shortlist=shortlist)


def reference(features, direction, active, shortlist):
    def one_group(group):
        group = group.astype(jnp.int32)
        vectors = direction[group]
        window = lax.dynamic_slice_in_dim(active, (group * LGROUP).astype(jnp.int32), LGROUP, 1)
        tiles = lax.dynamic_slice_in_dim(shortlist, (group * (LGROUP // TILE)).astype(jnp.int32), LGROUP // TILE, 1)
        blocks = window.reshape(ROWS // TILE, TILE, LGROUP // TILE, TILE) * tiles[:, None, :, None]
        weights = blocks.reshape(ROWS, LGROUP).astype(jnp.float32)
        margins = lax.dot_general(features, vectors, (((1,), (1,)), ((), ())), preferred_element_type=jnp.float32)
        scaled = (weights * margins).astype(jnp.bfloat16)
        row_total = lax.dot_general(scaled, features, (((0,), (0,)), ((), ())), preferred_element_type=jnp.float32)
        product = vectors.astype(jnp.float32) + row_total
        curve = jnp.sum(vectors.astype(jnp.float32) * product, axis=-1) / D
        return product, curve

    hess_product, curvature = lax.map(one_group, jnp.arange(N_LAB, dtype=jnp.int32))
    return hess_product, curvature
```

```python
import functools

import jax
import jax.numpy as jnp
from jax import lax
from jax.experimental import pallas as pl
from jax.experimental.pallas import tpu as pltpu
from jax.sharding import PartitionSpec as P

MESH = pl.DeviceIdType.MESH
CHUNKS = 2


def remote(src, dst, send, recv, **where):
    return pltpu.make_async_remote_copy(
        src_ref=src, dst_ref=dst, send_sem=send, recv_sem=recv, device_id=where, device_id_type=MESH
    )


def kernel(
    n_blk, n_lab, feats, dirs, active, short, hess, curve,
    slab, group, act, weights, scaled, acc, from_x, from_z,
    local_sem, y_send, y_recv, s_send, s_recv, f_send, f_recv,
    g_send, g_recv, x_send, x_recv, z_send, z_recv,
):
    rows, depth = feats.shape
    own = dirs.shape[1]
    n_z, n_pair = n_blk // 2, n_lab // 2
    labels = n_blk * own
    part = rows // CHUNKS
    blk, lab = lax.axis_index("blk"), lax.axis_index("lab")
    x, z = lax.rem(blk, 2), lax.div(blk, 2)
    core, pair = lax.rem(lab, 2), lax.div(lab, 2)
    x_peer = blk + 1 - 2 * x
    core_peer = lab + 1 - 2 * core

    local = [
        pltpu.make_async_copy(feats, slab.at[pair, core], local_sem.at[0]),
        pltpu.make_async_copy(dirs.at[0], group.at[x, z], local_sem.at[1]),
        pltpu.make_async_copy(active, act, local_sem.at[2]),
    ]
    for copy in local:
        copy.start()

    barrier = pltpu.get_barrier_semaphore()
    for k in range(1, n_blk):
        pl.semaphore_signal(barrier, inc=1, device_id={"blk": lax.rem(blk + k, n_blk)}, device_id_type=MESH)
    for k in range(1, n_pair):
        pl.semaphore_signal(
            barrier, inc=1, device_id={"lab": 2 * lax.rem(pair + k, n_pair) + core}, device_id_type=MESH
        )
    pl.semaphore_signal(barrier, inc=1, device_id={"lab": core_peer}, device_id_type=MESH)
    pl.semaphore_wait(barrier, n_blk - 1 + n_pair)

    sent = []

    def go(copy):
        copy.start()
        sent.append(copy)

    for c in range(CHUNKS):
        piece = pl.ds(c * part, part)
        for k in range(1, n_pair):
            go(remote(
                feats.at[piece], slab.at[pair, core, piece], y_send.at[k - 1, c], y_recv.at[k - 1, c],
                lab=2 * lax.rem(pair + k, n_pair) + core,
            ))
    for k in range(1, n_blk):
        go(remote(
            dirs.at[0], group.at[x, z], g_send.at[k - 1], g_recv.at[k - 1], blk=lax.rem(blk + k, n_blk)
        ))
    go(remote(feats, slab.at[pair, core], s_send.at[0], s_recv.at[0], lab=core_peer))

    local[2].wait()
    row_tile = active.shape[0] // short.shape[0]
    label_tile = active.shape[1] // short.shape[1]
    for r in range(short.shape[0]):
        for t in range(short.shape[1]):
            tile = act[r * row_tile:(r + 1) * row_tile, t * label_tile:(t + 1) * label_tile] * short[r, t]
            tile = tile.astype(jnp.float32).T
            at_pair, offset = divmod(r * row_tile, 2 * rows)
            for j in range(label_tile // own):
                device = t * (label_tile // own) + j
                slot = (device % 2) * n_z * own + (device // 2) * own
                weights[at_pair, slot:slot + own, offset:offset + row_tile] = tile[j * own:(j + 1) * own]

    for k in range(1, n_pair):
        source = lax.rem(pair + n_pair - k, n_pair)
        for c in range(CHUNKS):
            piece = pl.ds(c * part, part)
            block = slab.at[source, core, piece]
            remote(block, block, y_send.at[k - 1, c], y_recv.at[k - 1, c], lab=core_peer).wait_recv()
            go(remote(block, block, f_send.at[k - 1, c], f_recv.at[k - 1, c], lab=core_peer))

    local[0].wait()
    local[1].wait()
    other = slab.at[pair, 1 - core]
    remote(other, other, s_send.at[0], s_recv.at[0], lab=core_peer).wait_recv()
    for k in range(1, n_blk):
        source = lax.rem(blk + n_blk - k, n_blk)
        block = group.at[lax.rem(source, 2), lax.div(source, 2)]
        remote(block, block, g_send.at[k - 1], g_recv.at[k - 1], blk=x_peer).wait_recv()

    def masked(at):
        margins = lax.dot_general(
            group[...].reshape(labels, depth), slab[at].reshape(2 * rows, depth),
            (((1,), (1,)), ((), ())), preferred_element_type=jnp.float32,
        )
        return (weights[at] * margins).astype(jnp.bfloat16)

    def arrive(k):
        source = lax.rem(pair + n_pair - k, n_pair)
        for c in range(CHUNKS):
            block = slab.at[source, 1 - core, pl.ds(c * part, part)]
            remote(block, block, f_send.at[k - 1, c], f_recv.at[k - 1, c], lab=core_peer).wait_recv()
        return source

    def whole(at):
        return jnp.dot(
            masked(at), slab[at].reshape(2 * rows, depth), preferred_element_type=jnp.float32
        ).reshape(acc.shape)

    acc[...] = whole(pair)
    if n_pair > 2:
        @pl.loop(1, n_pair - 1)
        def _(k):
            acc[...] += whole(arrive(k))

    last = arrive(n_pair - 1)
    scaled[...] = masked(last).reshape(scaled.shape)

    def finish(half):
        acc[half] += jnp.dot(
            scaled[half], slab[last].reshape(2 * rows, depth), preferred_element_type=jnp.float32
        ).reshape(acc.shape[1:])

    finish(1 - x)
    for i in range(n_z):
        to = lax.rem(z + 1 + i, n_z)
        go(remote(acc.at[1 - x, to], from_x.at[to], x_send.at[i], x_recv.at[i], blk=x_peer))
    finish(x)
    for i in range(n_z):
        to = lax.rem(z + 1 + i, n_z)
        block = from_x.at[to]
        remote(block, block, x_send.at[i], x_recv.at[i], blk=x_peer).wait_recv()
        acc[x, to] += from_x[to]
        if i < n_z - 1:
            go(remote(acc.at[x, to], from_z.at[i], z_send.at[i], z_recv.at[i], blk=2 * to + x))

    vectors = group[x, z].astype(jnp.float32)
    total = acc[x, z]
    for i in range(n_z - 1):
        block = from_z.at[i]
        remote(block, block, z_send.at[i], z_recv.at[i], blk=x_peer).wait_recv()
        total += from_z[i]
    product = vectors + total
    hess[0] = product
    column = jnp.sum(vectors * product, axis=1, keepdims=True) / depth
    at_row = lax.broadcasted_iota(jnp.int32, (own, own), 0)
    at_column = lax.broadcasted_iota(jnp.int32, (own, own), 1)
    curve[...] = jnp.sum(jnp.where(at_row == at_column, column, 0.0), axis=0, keepdims=True)

    for copy in sent:
        copy.wait_send()


def solution(mesh):
    n_blk, n_lab = mesh.shape["blk"], mesh.shape["lab"]

    def shards(features, direction, active, shortlist):
        rows, depth = features.shape
        own = direction.shape[1]
        n_z, n_pair = n_blk // 2, n_lab // 2
        labels = n_blk * own
        dma = pltpu.SemaphoreType.DMA
        others = max(n_pair - 1, 1)
        scratch = [
            pltpu.VMEM((n_pair, 2, rows, depth), features.dtype),
            pltpu.VMEM((2, n_z, own, depth), direction.dtype),
            pltpu.VMEM(active.shape, active.dtype),
            pltpu.VMEM((n_pair, labels, 2 * rows), jnp.float32),
            pltpu.VMEM((2, n_z * own, 2 * rows), jnp.bfloat16),
            pltpu.VMEM((2, n_z, own, depth), jnp.float32),
            pltpu.VMEM((n_z, own, depth), jnp.float32),
            pltpu.VMEM((n_z - 1, own, depth), jnp.float32),
            dma((3,)),
            dma((others, CHUNKS)), dma((others, CHUNKS)),
            dma((1,)), dma((1,)),
            dma((others, CHUNKS)), dma((others, CHUNKS)),
            dma((n_blk - 1,)), dma((n_blk - 1,)),
            dma((n_z,)), dma((n_z,)),
            dma((n_z - 1,)), dma((n_z - 1,)),
        ]
        held = sum(
            functools.reduce(lambda a, b: a * b, s.shape) * jnp.dtype(s.dtype).itemsize for s in scratch[:8]
        )
        anywhere = pl.BlockSpec(memory_space=pl.ANY)
        vmem = pl.BlockSpec(memory_space=pltpu.VMEM)
        return pl.pallas_call(
            functools.partial(kernel, n_blk, n_lab),
            out_shape=(
                jax.ShapeDtypeStruct((1, own, depth), jnp.float32),
                jax.ShapeDtypeStruct((1, own), jnp.float32),
            ),
            in_specs=[anywhere, anywhere, anywhere, pl.BlockSpec(memory_space=pltpu.SMEM)],
            out_specs=(vmem, vmem),
            scratch_shapes=scratch,
            compiler_params=pltpu.CompilerParams(
                collective_id=0, has_side_effects=True, vmem_limit_bytes=2 * held + (8 << 20)
            ),
            name="hessian",
        )(features, direction, active, shortlist)

    return jax.shard_map(
        shards,
        mesh=mesh,
        in_specs=(P(("blk", "lab"), None), P("lab", "blk", None), P("blk", "lab"), P("blk", "lab")),
        out_specs=(P("lab", "blk", None), P("lab", "blk")),
        check_vma=False,
    )
```

```python
import functools

import jax
import jax.numpy as jnp
from jax import lax
from jax.experimental import pallas as pl
from jax.experimental.pallas import tpu as pltpu
from jax.sharding import PartitionSpec as P

MESH = pl.DeviceIdType.MESH
CHUNKS = 2
PIECES = 2


def remote(src, dst, send, recv, **where):
    return pltpu.make_async_remote_copy(
        src_ref=src, dst_ref=dst, send_sem=send, recv_sem=recv, device_id=where, device_id_type=MESH
    )


def kernel(
    n_blk, n_lab, feats, dirs, active, short, hess,
    slab, group, act, tiles, weights, scaled, acc, from_x, from_z,
    local_sem, y_send, y_recv, s_send, s_recv, f_send, f_recv,
    g_send, g_recv, h_send, h_recv, x_send, x_recv, z_send, z_recv,
):
    rows, depth = feats.shape
    own = dirs.shape[1]
    n_z, n_pair = n_blk // 2, n_lab // 2
    labels = n_blk * own
    part = rows // CHUNKS
    blk, lab = lax.axis_index("blk"), lax.axis_index("lab")
    x, z = lax.rem(blk, 2), lax.div(blk, 2)
    core, pair = lax.rem(lab, 2), lax.div(lab, 2)
    x_peer = blk + 1 - 2 * x
    core_peer = lab + 1 - 2 * core

    local = [
        pltpu.make_async_copy(feats, slab.at[pair, core], local_sem.at[0]),
        pltpu.make_async_copy(dirs.at[0], group.at[x, z], local_sem.at[1]),
        pltpu.make_async_copy(active, act, local_sem.at[2]),
        pltpu.make_async_copy(short, tiles, local_sem.at[3]),
    ]
    for copy in local:
        copy.start()

    barrier = pltpu.get_barrier_semaphore()
    for k in range(1, n_z):
        pl.semaphore_signal(
            barrier, inc=1, device_id={"blk": 2 * lax.rem(z + k, n_z) + x}, device_id_type=MESH
        )
    pl.semaphore_signal(barrier, inc=1, device_id={"blk": x_peer}, device_id_type=MESH)
    for k in range(1, n_pair):
        pl.semaphore_signal(
            barrier, inc=1, device_id={"lab": 2 * lax.rem(pair + k, n_pair) + core}, device_id_type=MESH
        )
    pl.semaphore_signal(barrier, inc=1, device_id={"lab": core_peer}, device_id_type=MESH)
    pl.semaphore_wait(barrier, n_z + n_pair)

    sent = []

    def go(copy):
        copy.start()
        sent.append(copy)

    for c in range(CHUNKS):
        piece = pl.ds(c * part, part)
        for k in range(1, n_pair):
            go(remote(
                feats.at[piece], slab.at[pair, core, piece], y_send.at[k - 1, c], y_recv.at[k - 1, c],
                lab=2 * lax.rem(pair + k, n_pair) + core,
            ))
    for k in range(1, n_z):
        go(remote(
            dirs.at[0], group.at[x, z], g_send.at[k - 1], g_recv.at[k - 1], blk=2 * lax.rem(z + k, n_z) + x
        ))
    go(remote(dirs.at[0], group.at[x, z], h_send.at[0], h_recv.at[0], blk=x_peer))
    go(remote(feats, slab.at[pair, core], s_send.at[0], s_recv.at[0], lab=core_peer))

    local[2].wait()
    local[3].wait()
    row_tile = active.shape[0] // short.shape[1]
    label_tile = active.shape[1] // short.shape[0]
    for r in range(short.shape[1]):
        for t in range(short.shape[0]):
            tile = act[r * row_tile:(r + 1) * row_tile, t * label_tile:(t + 1) * label_tile] * tiles[t:t + 1, r:r + 1]
            tile = tile.astype(jnp.float32).T
            at_pair, offset = divmod(r * row_tile, 2 * rows)
            for j in range(label_tile // own):
                device = t * (label_tile // own) + j
                slot = (device % 2) * n_z * own + (device // 2) * own
                weights[at_pair, slot:slot + own, offset:offset + row_tile] = tile[j * own:(j + 1) * own]

    for k in range(1, n_z):
        block = group.at[x, lax.rem(z + n_z - k, n_z)]
        remote(block, block, g_send.at[k - 1], g_recv.at[k - 1], blk=x_peer).wait_recv()
        go(remote(block, block, h_send.at[k], h_recv.at[k], blk=x_peer))

    def pass_on(c):
        for k in range(1, n_pair):
            block = slab.at[lax.rem(pair + n_pair - k, n_pair), core, pl.ds(c * part, part)]
            remote(block, block, y_send.at[k - 1, c], y_recv.at[k - 1, c], lab=core_peer).wait_recv()
            go(remote(block, block, f_send.at[k - 1, c], f_recv.at[k - 1, c], lab=core_peer))

    for c in range(CHUNKS - 1):
        pass_on(c)
    local[0].wait()
    local[1].wait()
    other = slab.at[pair, 1 - core]
    remote(other, other, s_send.at[0], s_recv.at[0], lab=core_peer).wait_recv()
    for k in range(n_z):
        block = group.at[1 - x, lax.rem(z + n_z - k, n_z)]
        remote(block, block, h_send.at[k], h_recv.at[k], blk=x_peer).wait_recv()

    def masked(at):
        margins = lax.dot_general(
            group[...].reshape(labels, depth), slab[at].reshape(2 * rows, depth),
            (((1,), (1,)), ((), ())), preferred_element_type=jnp.float32,
        )
        return (weights[at] * margins).astype(jnp.bfloat16)

    def arrive(k):
        source = lax.rem(pair + n_pair - k, n_pair)
        for c in range(CHUNKS):
            block = slab.at[source, 1 - core, pl.ds(c * part, part)]
            remote(block, block, f_send.at[k - 1, c], f_recv.at[k - 1, c], lab=core_peer).wait_recv()
        return source

    def whole(at):
        return jnp.dot(
            masked(at), slab[at].reshape(2 * rows, depth), preferred_element_type=jnp.float32
        ).reshape(acc.shape)

    acc[...] = whole(pair)
    pass_on(CHUNKS - 1)
    if n_pair > 2:
        @pl.loop(1, n_pair - 1)
        def _(k):
            acc[...] += whole(arrive(k))

    last = arrive(n_pair - 1)
    scaled[...] = masked(last).reshape(scaled.shape)

    def finish(half):
        acc[half] += jnp.dot(
            scaled[half], slab[last].reshape(2 * rows, depth), preferred_element_type=jnp.float32
        ).reshape(acc.shape[1:])

    finish(1 - x)
    step = own // PIECES
    for i in range(n_z):
        to = lax.rem(z + 1 + i, n_z)
        for c in range(PIECES):
            piece = pl.ds(c * step, step)
            go(remote(
                acc.at[1 - x, to, piece], from_x.at[to, piece], x_send.at[i, c], x_recv.at[i, c], blk=x_peer
            ))
    finish(x)
    for i in range(n_z):
        to = lax.rem(z + 1 + i, n_z)
        for c in range(PIECES):
            piece = pl.ds(c * step, step)
            block = from_x.at[to, piece]
            remote(block, block, x_send.at[i, c], x_recv.at[i, c], blk=x_peer).wait_recv()
            acc[x, to, piece] += from_x[to, piece]
            if i < n_z - 1:
                go(remote(
                    acc.at[x, to, piece], from_z.at[i, piece], z_send.at[i, c], z_recv.at[i, c], blk=2 * to + x
                ))

    vectors = group[x, z].astype(jnp.float32)
    total = acc[x, z]
    for i in range(n_z - 1):
        for c in range(PIECES):
            block = from_z.at[i, pl.ds(c * step, step)]
            remote(block, block, z_send.at[i, c], z_recv.at[i, c], blk=x_peer).wait_recv()
        total += from_z[i]
    product = vectors + total
    hess[0, :own] = product
    column = jnp.sum(vectors * product, axis=1, keepdims=True) / depth
    at_row = lax.broadcasted_iota(jnp.int32, (own, own), 0)
    at_column = lax.broadcasted_iota(jnp.int32, (own, own), 1)
    hess[0, own:own + 1, :own] = jnp.sum(jnp.where(at_row == at_column, column, 0.0), axis=0, keepdims=True)

    for copy in sent:
        copy.wait_send()


def solution(mesh):
    n_blk, n_lab = mesh.shape["blk"], mesh.shape["lab"]

    def shards(features, direction, active, shortlist):
        rows, depth = features.shape
        own = direction.shape[1]
        n_z, n_pair = n_blk // 2, n_lab // 2
        labels = n_blk * own
        dma = pltpu.SemaphoreType.DMA
        others = max(n_pair - 1, 1)
        scratch = [
            pltpu.VMEM((n_pair, 2, rows, depth), features.dtype),
            pltpu.VMEM((2, n_z, own, depth), direction.dtype),
            pltpu.VMEM(active.shape, active.dtype),
            pltpu.VMEM(shortlist.shape[::-1], shortlist.dtype),
            pltpu.VMEM((n_pair, labels, 2 * rows), jnp.float32),
            pltpu.VMEM((2, n_z * own, 2 * rows), jnp.bfloat16),
            pltpu.VMEM((2, n_z, own, depth), jnp.float32),
            pltpu.VMEM((n_z, own, depth), jnp.float32),
            pltpu.VMEM((n_z - 1, own, depth), jnp.float32),
            dma((4,)),
            dma((others, CHUNKS)), dma((others, CHUNKS)),
            dma((1,)), dma((1,)),
            dma((others, CHUNKS)), dma((others, CHUNKS)),
            dma((n_z - 1,)), dma((n_z - 1,)),
            dma((n_z,)), dma((n_z,)),
            dma((n_z, PIECES)), dma((n_z, PIECES)),
            dma((n_z - 1, PIECES)), dma((n_z - 1, PIECES)),
        ]
        hbm = pl.BlockSpec(memory_space=pltpu.HBM)
        vmem = pl.BlockSpec(memory_space=pltpu.VMEM)
        out, = pl.pallas_call(
            functools.partial(kernel, n_blk, n_lab),
            out_shape=(
                jax.ShapeDtypeStruct((1, own + 8, depth), jnp.float32),
            ),
            in_specs=[hbm, hbm, hbm, hbm],
            out_specs=(vmem,),
            scratch_shapes=scratch,
            compiler_params=pltpu.CompilerParams(
                collective_id=0, has_side_effects=True, vmem_limit_bytes=60 << 20
            ),
            name="hessian",
        )(features, direction, active, shortlist.T)
        return out[:, :own], out[:, own, :own]

    return jax.shard_map(
        shards,
        mesh=mesh,
        in_specs=(P(("blk", "lab"), None), P("lab", "blk", None), P("blk", "lab"), P("blk", "lab")),
        out_specs=(P("lab", "blk", None), P("lab", "blk")),
        check_vma=False,
    )
```

```python
import functools

import jax
import jax.numpy as jnp
from jax import lax
from jax.experimental import pallas as pl
from jax.experimental.pallas import tpu as pltpu
from jax.sharding import PartitionSpec as P

MESH = pl.DeviceIdType.MESH
CHUNKS = 2
PIECES = 2


def remote(src, dst, send, recv, **where):
    return pltpu.make_async_remote_copy(
        src_ref=src, dst_ref=dst, send_sem=send, recv_sem=recv, device_id=where, device_id_type=MESH
    )


def kernel(
    n_blk, n_lab, feats, dirs, active, short, hess, curve,
    slab, group, act, tiles, weights, scaled, acc, from_x, from_z,
    local_sem, y_send, y_recv, s_send, s_recv, f_send, f_recv,
    g_send, g_recv, h_send, h_recv, x_send, x_recv, z_send, z_recv,
):
    rows, depth = feats.shape
    own = dirs.shape[1]
    n_z, n_pair = n_blk // 2, n_lab // 2
    labels = n_blk * own
    part = rows // CHUNKS
    blk, lab = lax.axis_index("blk"), lax.axis_index("lab")
    x, z = lax.rem(blk, 2), lax.div(blk, 2)
    core, pair = lax.rem(lab, 2), lax.div(lab, 2)
    x_peer = blk + 1 - 2 * x
    core_peer = lab + 1 - 2 * core

    local = [
        pltpu.make_async_copy(feats, slab.at[pair, core], local_sem.at[0]),
        pltpu.make_async_copy(dirs.at[0], group.at[x, z], local_sem.at[1]),
        pltpu.make_async_copy(active, act, local_sem.at[2]),
        pltpu.make_async_copy(short, tiles, local_sem.at[3]),
    ]
    for copy in local:
        copy.start()

    barrier = pltpu.get_barrier_semaphore()
    for k in range(1, n_z):
        pl.semaphore_signal(
            barrier, inc=1, device_id={"blk": 2 * lax.rem(z + k, n_z) + x}, device_id_type=MESH
        )
    pl.semaphore_signal(barrier, inc=1, device_id={"blk": x_peer}, device_id_type=MESH)
    for k in range(1, n_pair):
        pl.semaphore_signal(
            barrier, inc=1, device_id={"lab": 2 * lax.rem(pair + k, n_pair) + core}, device_id_type=MESH
        )
    pl.semaphore_signal(barrier, inc=1, device_id={"lab": core_peer}, device_id_type=MESH)
    pl.semaphore_wait(barrier, n_z + n_pair)

    sent = []

    def go(copy):
        copy.start()
        sent.append(copy)

    for c in range(CHUNKS):
        piece = pl.ds(c * part, part)
        for k in range(1, n_pair):
            go(remote(
                feats.at[piece], slab.at[pair, core, piece], y_send.at[k - 1, c], y_recv.at[k - 1, c],
                lab=2 * lax.rem(pair + k, n_pair) + core,
            ))
    for k in range(1, n_z):
        go(remote(
            dirs.at[0], group.at[x, z], g_send.at[k - 1], g_recv.at[k - 1], blk=2 * lax.rem(z + k, n_z) + x
        ))
    go(remote(dirs.at[0], group.at[x, z], h_send.at[0], h_recv.at[0], blk=x_peer))
    go(remote(feats, slab.at[pair, core], s_send.at[0], s_recv.at[0], lab=core_peer))

    local[2].wait()
    local[3].wait()
    row_tile = active.shape[0] // short.shape[1]
    label_tile = active.shape[1] // short.shape[0]
    for r in range(short.shape[1]):
        for t in range(short.shape[0]):
            tile = act[r * row_tile:(r + 1) * row_tile, t * label_tile:(t + 1) * label_tile] * tiles[t:t + 1, r:r + 1]
            tile = tile.astype(jnp.float32).T
            block, offset = divmod(r * row_tile, rows)
            for j in range(label_tile // own):
                device = t * (label_tile // own) + j
                slot = (device % 2) * n_z * own + (device // 2) * own
                weights[block // 2, block % 2, slot:slot + own, offset:offset + row_tile] = tile[j * own:(j + 1) * own]

    for k in range(1, n_z):
        block = group.at[x, lax.rem(z + n_z - k, n_z)]
        remote(block, block, g_send.at[k - 1], g_recv.at[k - 1], blk=x_peer).wait_recv()
        go(remote(block, block, h_send.at[k], h_recv.at[k], blk=x_peer))

    def pass_on(c):
        for k in range(1, n_pair):
            block = slab.at[lax.rem(pair + n_pair - k, n_pair), core, pl.ds(c * part, part)]
            remote(block, block, y_send.at[k - 1, c], y_recv.at[k - 1, c], lab=core_peer).wait_recv()
            go(remote(block, block, f_send.at[k - 1, c], f_recv.at[k - 1, c], lab=core_peer))

    for c in range(CHUNKS):
        pass_on(c)
    local[0].wait()
    local[1].wait()
    for k in range(n_z):
        block = group.at[1 - x, lax.rem(z + n_z - k, n_z)]
        remote(block, block, h_send.at[k], h_recv.at[k], blk=x_peer).wait_recv()

    def masked(at, side):
        margins = lax.dot_general(
            group[...].reshape(labels, depth), slab[at, side],
            (((1,), (1,)), ((), ())), preferred_element_type=jnp.float32,
        )
        return (weights[at, side] * margins).astype(jnp.bfloat16)

    def whole(at, side):
        return jnp.dot(
            masked(at, side), slab[at, side], preferred_element_type=jnp.float32
        ).reshape(acc.shape)

    def arrive(k):
        source = lax.rem(pair + n_pair - k, n_pair)
        for c in range(CHUNKS):
            block = slab.at[source, 1 - core, pl.ds(c * part, part)]
            remote(block, block, f_send.at[k - 1, c], f_recv.at[k - 1, c], lab=core_peer).wait_recv()

    acc[...] = whole(pair, core)
    other = slab.at[pair, 1 - core]
    remote(other, other, s_send.at[0], s_recv.at[0], lab=core_peer).wait_recv()
    acc[...] += whole(pair, 1 - core)
    if n_pair > 2:
        @pl.loop(1, n_pair - 1)
        def _(k):
            source = lax.rem(pair + n_pair - k, n_pair)
            acc[...] += whole(source, core)
            arrive(k)
            acc[...] += whole(source, 1 - core)

    last = lax.rem(pair + 1, n_pair)
    acc[...] += whole(last, core)
    arrive(n_pair - 1)
    scaled[...] = masked(last, 1 - core).reshape(scaled.shape)

    def finish(half):
        acc[half] += jnp.dot(
            scaled[half], slab[last, 1 - core], preferred_element_type=jnp.float32
        ).reshape(acc.shape[1:])

    finish(1 - x)
    step = own // PIECES
    for i in range(n_z):
        to = lax.rem(z + 1 + i, n_z)
        for c in range(PIECES):
            piece = pl.ds(c * step, step)
            go(remote(
                acc.at[1 - x, to, piece], from_x.at[to, piece], x_send.at[i, c], x_recv.at[i, c], blk=x_peer
            ))
    finish(x)
    for i in range(n_z):
        to = lax.rem(z + 1 + i, n_z)
        for c in range(PIECES):
            piece = pl.ds(c * step, step)
            block = from_x.at[to, piece]
            remote(block, block, x_send.at[i, c], x_recv.at[i, c], blk=x_peer).wait_recv()
            acc[x, to, piece] += from_x[to, piece]
            if i < n_z - 1:
                go(remote(
                    acc.at[x, to, piece], from_z.at[i, piece], z_send.at[i, c], z_recv.at[i, c], blk=2 * to + x
                ))

    vectors = group[x, z].astype(jnp.float32)
    total = acc[x, z]
    for i in range(n_z - 1):
        for c in range(PIECES):
            block = from_z.at[i, pl.ds(c * step, step)]
            remote(block, block, z_send.at[i, c], z_recv.at[i, c], blk=x_peer).wait_recv()
        total += from_z[i]
    product = vectors + total
    hess[0] = product
    column = jnp.sum(vectors * product, axis=1, keepdims=True) / depth
    at_row = lax.broadcasted_iota(jnp.int32, (own, own), 0)
    at_column = lax.broadcasted_iota(jnp.int32, (own, own), 1)
    curve[...] = jnp.sum(jnp.where(at_row == at_column, column, 0.0), axis=0, keepdims=True)

    for copy in sent:
        copy.wait_send()


def solution(mesh):
    n_blk, n_lab = mesh.shape["blk"], mesh.shape["lab"]

    def shards(features, direction, active, shortlist):
        rows, depth = features.shape
        own = direction.shape[1]
        n_z, n_pair = n_blk // 2, n_lab // 2
        labels = n_blk * own
        dma = pltpu.SemaphoreType.DMA
        others = max(n_pair - 1, 1)
        scratch = [
            pltpu.VMEM((n_pair, 2, rows, depth), features.dtype),
            pltpu.VMEM((2, n_z, own, depth), direction.dtype),
            pltpu.VMEM(active.shape, active.dtype),
            pltpu.VMEM(shortlist.shape[::-1], shortlist.dtype),
            pltpu.VMEM((n_pair, 2, labels, rows), jnp.float32),
            pltpu.VMEM((2, n_z * own, rows), jnp.bfloat16),
            pltpu.VMEM((2, n_z, own, depth), jnp.float32),
            pltpu.VMEM((n_z, own, depth), jnp.float32),
            pltpu.VMEM((n_z - 1, own, depth), jnp.float32),
            dma((4,)),
            dma((others, CHUNKS)), dma((others, CHUNKS)),
            dma((1,)), dma((1,)),
            dma((others, CHUNKS)), dma((others, CHUNKS)),
            dma((n_z - 1,)), dma((n_z - 1,)),
            dma((n_z,)), dma((n_z,)),
            dma((n_z, PIECES)), dma((n_z, PIECES)),
            dma((n_z - 1, PIECES)), dma((n_z - 1, PIECES)),
        ]
        hbm = pl.BlockSpec(memory_space=pltpu.HBM)
        vmem = pl.BlockSpec(memory_space=pltpu.VMEM)
        return pl.pallas_call(
            functools.partial(kernel, n_blk, n_lab),
            out_shape=(
                pltpu.VMEM((1, own, depth), jnp.float32),
                pltpu.VMEM((1, own), jnp.float32),
            ),
            in_specs=[hbm, hbm, hbm, hbm],
            out_specs=(vmem, vmem),
            scratch_shapes=scratch,
            compiler_params=pltpu.CompilerParams(
                collective_id=0, has_side_effects=True, vmem_limit_bytes=60 << 20
            ),
            name="hessian",
        )(features, direction, active, shortlist.T)

    return jax.shard_map(
        shards,
        mesh=mesh,
        in_specs=(P(("blk", "lab"), None), P("lab", "blk", None), P("blk", "lab"), P("blk", "lab")),
        out_specs=(P("lab", "blk", None), P("lab", "blk")),
        check_vma=False,
    )
```

```python
import functools

import jax
import jax.numpy as jnp
from jax import lax
from jax.experimental import pallas as pl
from jax.experimental.pallas import tpu as pltpu
from jax.sharding import PartitionSpec as P

MESH = pl.DeviceIdType.MESH
TAIL = 16
PIECES = 2


def remote(src, dst, send, recv, **where):
    return pltpu.make_async_remote_copy(
        src_ref=src, dst_ref=dst, send_sem=send, recv_sem=recv, device_id=where, device_id_type=MESH
    )


def kernel(
    n_blk, n_lab, feats, dirs, active, short, hess, curve,
    slab, group, act, tiles, weights, acc, from_x, from_z,
    local_sem, y_send, y_recv, s_send, s_recv, f_send, f_recv,
    g_send, g_recv, h_send, h_recv, x_send, x_recv, z_send, z_recv,
):
    rows, depth = feats.shape
    own = dirs.shape[1]
    n_z, n_pair = n_blk // 2, n_lab // 2
    labels = n_blk * own
    cuts = (pl.ds(0, rows // 2), pl.ds(rows // 2, rows // 2 - TAIL), pl.ds(rows - TAIL, TAIL))
    blk, lab = lax.axis_index("blk"), lax.axis_index("lab")
    x, z = lax.rem(blk, 2), lax.div(blk, 2)
    core, pair = lax.rem(lab, 2), lax.div(lab, 2)
    x_peer = blk + 1 - 2 * x
    core_peer = lab + 1 - 2 * core

    local = [
        pltpu.make_async_copy(feats, slab.at[pair, core], local_sem.at[0]),
        pltpu.make_async_copy(dirs.at[0], group.at[x, z], local_sem.at[1]),
        pltpu.make_async_copy(active, act, local_sem.at[2]),
        pltpu.make_async_copy(short, tiles, local_sem.at[3]),
    ]
    barrier = pltpu.get_barrier_semaphore()
    for k in range(1, n_z):
        pl.semaphore_signal(
            barrier, inc=1, device_id={"blk": 2 * lax.rem(z + k, n_z) + x}, device_id_type=MESH
        )
    pl.semaphore_signal(barrier, inc=1, device_id={"blk": x_peer}, device_id_type=MESH)
    for k in range(1, n_pair):
        for side in range(2):
            pl.semaphore_signal(
                barrier, inc=1, device_id={"lab": 2 * lax.rem(pair + k, n_pair) + side}, device_id_type=MESH
            )
    pl.semaphore_signal(barrier, inc=1, device_id={"lab": core_peer}, device_id_type=MESH)
    for copy in local:
        copy.start()
    pl.semaphore_wait(barrier, n_z + 2 * n_pair - 1)

    sent = []

    def go(copy):
        copy.start()
        sent.append(copy)

    for c, piece in enumerate(cuts):
        for k in range(1, n_pair):
            to = 2 * lax.rem(pair + k, n_pair)
            go(remote(
                feats.at[piece], slab.at[pair, core, piece], y_send.at[k - 1, c], y_recv.at[k - 1, c],
                lab=to + core,
            ))
            if c == len(cuts) - 1:
                go(remote(
                    feats.at[piece], slab.at[pair, core, piece], f_send.at[k - 1, c], f_recv.at[k - 1, c],
                    lab=to + 1 - core,
                ))
    for k in range(1, n_z):
        go(remote(
            dirs.at[0], group.at[x, z], g_send.at[k - 1], g_recv.at[k - 1], blk=2 * lax.rem(z + k, n_z) + x
        ))
    go(remote(dirs.at[0], group.at[x, z], h_send.at[0], h_recv.at[0], blk=x_peer))
    go(remote(feats, slab.at[pair, core], s_send.at[0], s_recv.at[0], lab=core_peer))

    local[2].wait()
    local[3].wait()
    row_tile = active.shape[0] // short.shape[1]
    label_tile = active.shape[1] // short.shape[0]
    for r in range(short.shape[1]):
        for t in range(short.shape[0]):
            tile = act[r * row_tile:(r + 1) * row_tile, t * label_tile:(t + 1) * label_tile] * tiles[t:t + 1, r:r + 1]
            tile = tile.astype(jnp.float32).T
            block, offset = divmod(r * row_tile, rows)
            for j in range(label_tile // own):
                device = t * (label_tile // own) + j
                slot = (device // 2) * own
                weights[block // 2, block % 2, device % 2, slot:slot + own, offset:offset + row_tile] = tile[j * own:(j + 1) * own]

    for k in range(1, n_z):
        block = group.at[x, lax.rem(z + n_z - k, n_z)]
        remote(block, block, g_send.at[k - 1], g_recv.at[k - 1], blk=x_peer).wait_recv()
        go(remote(block, block, h_send.at[k], h_recv.at[k], blk=x_peer))

    def direct(k, c):
        block = slab.at[lax.rem(pair + n_pair - k, n_pair), core, cuts[c]]
        remote(block, block, y_send.at[k - 1, c], y_recv.at[k - 1, c], lab=core_peer).wait_recv()
        return block

    for c in range(len(cuts) - 1):
        for k in range(1, n_pair):
            block = direct(k, c)
            go(remote(block, block, f_send.at[k - 1, c], f_recv.at[k - 1, c], lab=core_peer))
    local[0].wait()
    local[1].wait()
    for k in range(n_z):
        block = group.at[1 - x, lax.rem(z + n_z - k, n_z)]
        remote(block, block, h_send.at[k], h_recv.at[k], blk=x_peer).wait_recv()

    def term(vectors, mask, block):
        margins = lax.dot_general(
            vectors, block, (((1,), (1,)), ((), ())), preferred_element_type=jnp.float32
        )
        return jnp.dot((mask * margins).astype(jnp.bfloat16), block, preferred_element_type=jnp.float32)

    def whole(at, side):
        return term(
            group[...].reshape(labels, depth), weights[at, side].reshape(labels, rows), slab[at, side]
        ).reshape(acc.shape)

    def arrive(k):
        source = lax.rem(pair + n_pair - k, n_pair)
        for c, piece in enumerate(cuts):
            block = slab.at[source, 1 - core, piece]
            remote(block, block, f_send.at[k - 1, c], f_recv.at[k - 1, c], lab=core_peer).wait_recv()

    acc[...] = whole(pair, core)
    other = slab.at[pair, 1 - core]
    remote(other, other, s_send.at[0], s_recv.at[0], lab=core_peer).wait_recv()
    acc[...] += whole(pair, 1 - core)
    if n_pair > 2:
        @pl.loop(1, n_pair - 1)
        def _(k):
            source = lax.rem(pair + n_pair - k, n_pair)
            direct(k, len(cuts) - 1)
            acc[...] += whole(source, core)
            arrive(k)
            acc[...] += whole(source, 1 - core)

    last = lax.rem(pair + 1, n_pair)
    direct(n_pair - 1, len(cuts) - 1)
    acc[...] += whole(last, core)
    arrive(n_pair - 1)

    def finish(half):
        acc[half] += term(
            group[half].reshape(labels // 2, depth), weights[last, 1 - core, half], slab[last, 1 - core]
        ).reshape(acc.shape[1:])

    finish(1 - x)
    step = own // PIECES
    for i in range(n_z):
        to = lax.rem(z + 1 + i, n_z)
        for c in range(PIECES):
            piece = pl.ds(c * step, step)
            go(remote(
                acc.at[1 - x, to, piece], from_x.at[to, piece], x_send.at[i, c], x_recv.at[i, c], blk=x_peer
            ))
    finish(x)
    for i in range(n_z):
        to = lax.rem(z + 1 + i, n_z)
        for c in range(PIECES):
            piece = pl.ds(c * step, step)
            block = from_x.at[to, piece]
            remote(block, block, x_send.at[i, c], x_recv.at[i, c], blk=x_peer).wait_recv()
            acc[x, to, piece] += from_x[to, piece]
            if i < n_z - 1:
                go(remote(
                    acc.at[x, to, piece], from_z.at[i, piece], z_send.at[i, c], z_recv.at[i, c], blk=2 * to + x
                ))

    vectors = group[x, z].astype(jnp.float32)
    total = acc[x, z]
    for i in range(n_z - 1):
        for c in range(PIECES):
            block = from_z.at[i, pl.ds(c * step, step)]
            remote(block, block, z_send.at[i, c], z_recv.at[i, c], blk=x_peer).wait_recv()
        total += from_z[i]
    product = vectors + total
    hess[0] = product
    column = jnp.sum(vectors * product, axis=1, keepdims=True) / depth
    at_row = lax.broadcasted_iota(jnp.int32, (own, own), 0)
    at_column = lax.broadcasted_iota(jnp.int32, (own, own), 1)
    curve[...] = jnp.sum(jnp.where(at_row == at_column, column, 0.0), axis=0, keepdims=True)

    for copy in sent:
        copy.wait_send()


def solution(mesh):
    n_blk, n_lab = mesh.shape["blk"], mesh.shape["lab"]

    def shards(features, direction, active, shortlist):
        rows, depth = features.shape
        own = direction.shape[1]
        n_z, n_pair = n_blk // 2, n_lab // 2
        labels = n_blk * own
        dma = pltpu.SemaphoreType.DMA
        others = max(n_pair - 1, 1)
        scratch = [
            pltpu.VMEM((n_pair, 2, rows, depth), features.dtype),
            pltpu.VMEM((2, n_z, own, depth), direction.dtype),
            pltpu.VMEM(active.shape, active.dtype),
            pltpu.VMEM(shortlist.shape[::-1], shortlist.dtype),
            pltpu.VMEM((n_pair, 2, 2, labels // 2, rows), jnp.float32),
            pltpu.VMEM((2, n_z, own, depth), jnp.float32),
            pltpu.VMEM((n_z, own, depth), jnp.float32),
            pltpu.VMEM((n_z - 1, own, depth), jnp.float32),
            dma((4,)),
            dma((others, 3)), dma((others, 3)),
            dma((1,)), dma((1,)),
            dma((others, 3)), dma((others, 3)),
            dma((n_z - 1,)), dma((n_z - 1,)),
            dma((n_z,)), dma((n_z,)),
            dma((n_z, PIECES)), dma((n_z, PIECES)),
            dma((n_z - 1, PIECES)), dma((n_z - 1, PIECES)),
        ]
        hbm = pl.BlockSpec(memory_space=pltpu.HBM)
        vmem = pl.BlockSpec(memory_space=pltpu.VMEM)
        return pl.pallas_call(
            functools.partial(kernel, n_blk, n_lab),
            out_shape=(
                pltpu.VMEM((1, own, depth), jnp.float32),
                pltpu.VMEM((1, own), jnp.float32),
            ),
            in_specs=[hbm, hbm, hbm, hbm],
            out_specs=(vmem, vmem),
            scratch_shapes=scratch,
            compiler_params=pltpu.CompilerParams(
                collective_id=0, has_side_effects=True, vmem_limit_bytes=60 << 20
            ),
            name="hessian",
        )(features, direction, active, shortlist.T)

    return jax.shard_map(
        shards,
        mesh=mesh,
        in_specs=(P(("blk", "lab"), None), P("lab", "blk", None), P("blk", "lab"), P("blk", "lab")),
        out_specs=(P("lab", "blk", None), P("lab", "blk")),
        check_vma=False,
    )
```

```python
import functools

import jax
import jax.numpy as jnp
from jax import lax
from jax.experimental import pallas as pl
from jax.experimental.pallas import tpu as pltpu
from jax.sharding import PartitionSpec as P

MESH = pl.DeviceIdType.MESH
TAIL = 16
PIECES = 2


def remote(src, dst, send, recv, **where):
    return pltpu.make_async_remote_copy(
        src_ref=src, dst_ref=dst, send_sem=send, recv_sem=recv, device_id=where, device_id_type=MESH
    )


def kernel(
    n_blk, n_lab, feats, dirs, active, short, hess, curve,
    slab, group, act, tiles, weights, acc, from_x, from_z,
    local_sem, y_send, y_recv, s_send, s_recv, f_send, f_recv,
    g_send, g_recv, h_send, h_recv, x_send, x_recv, z_send, z_recv,
):
    rows, depth = feats.shape
    own = dirs.shape[1]
    n_z, n_pair = n_blk // 2, n_lab // 2
    labels = n_blk * own
    cuts = (pl.ds(0, rows - TAIL), pl.ds(rows - TAIL, TAIL))
    blk, lab = lax.axis_index("blk"), lax.axis_index("lab")
    x, z = lax.rem(blk, 2), lax.div(blk, 2)
    core, pair = lax.rem(lab, 2), lax.div(lab, 2)
    x_peer = blk + 1 - 2 * x
    core_peer = lab + 1 - 2 * core

    local = [
        pltpu.make_async_copy(feats, slab.at[pair, core], local_sem.at[0]),
        pltpu.make_async_copy(dirs.at[0], group.at[x, z], local_sem.at[1]),
        pltpu.make_async_copy(active, act, local_sem.at[2]),
        pltpu.make_async_copy(short, tiles, local_sem.at[3]),
    ]
    barrier = pltpu.get_barrier_semaphore()
    for k in range(1, n_z):
        pl.semaphore_signal(
            barrier, inc=1, device_id={"blk": 2 * lax.rem(z + k, n_z) + x}, device_id_type=MESH
        )
    pl.semaphore_signal(barrier, inc=1, device_id={"blk": x_peer}, device_id_type=MESH)
    for k in range(1, n_pair):
        for side in range(2):
            pl.semaphore_signal(
                barrier, inc=1, device_id={"lab": 2 * lax.rem(pair + k, n_pair) + side}, device_id_type=MESH
            )
    pl.semaphore_signal(barrier, inc=1, device_id={"lab": core_peer}, device_id_type=MESH)
    for copy in local:
        copy.start()
    pl.semaphore_wait(barrier, n_z + 2 * n_pair - 1)

    sent = []

    def go(copy):
        copy.start()
        sent.append(copy)

    for k in range(1, n_z):
        go(remote(
            dirs.at[0], group.at[x, z], g_send.at[k - 1], g_recv.at[k - 1], blk=2 * lax.rem(z + k, n_z) + x
        ))
    go(remote(dirs.at[0], group.at[x, z], h_send.at[0], h_recv.at[0], blk=x_peer))
    for c, piece in enumerate(cuts):
        for k in range(1, n_pair):
            to = 2 * lax.rem(pair + k, n_pair)
            go(remote(
                feats.at[piece], slab.at[pair, core, piece], y_send.at[k - 1, c], y_recv.at[k - 1, c],
                lab=to + core,
            ))
            if c == len(cuts) - 1:
                go(remote(
                    feats.at[piece], slab.at[pair, core, piece], f_send.at[k - 1, c], f_recv.at[k - 1, c],
                    lab=to + 1 - core,
                ))
    go(remote(feats, slab.at[pair, core], s_send.at[0], s_recv.at[0], lab=core_peer))

    local[2].wait()
    local[3].wait()
    row_tile = active.shape[0] // short.shape[1]
    label_tile = active.shape[1] // short.shape[0]
    for r in range(short.shape[1]):
        for t in range(short.shape[0]):
            tile = act[r * row_tile:(r + 1) * row_tile, t * label_tile:(t + 1) * label_tile] * tiles[t:t + 1, r:r + 1]
            tile = tile.astype(jnp.float32).T
            at_pair, offset = divmod(r * row_tile, 2 * rows)
            for j in range(label_tile // own):
                device = t * (label_tile // own) + j
                slot = (device // 2) * own
                weights[at_pair, device % 2, slot:slot + own, offset:offset + row_tile] = tile[j * own:(j + 1) * own]

    for k in range(1, n_z):
        block = group.at[x, lax.rem(z + n_z - k, n_z)]
        remote(block, block, g_send.at[k - 1], g_recv.at[k - 1], blk=x_peer).wait_recv()
        go(remote(block, block, h_send.at[k], h_recv.at[k], blk=x_peer))

    def direct(k, c):
        block = slab.at[lax.rem(pair + n_pair - k, n_pair), core, cuts[c]]
        remote(block, block, y_send.at[k - 1, c], y_recv.at[k - 1, c], lab=core_peer).wait_recv()
        return block

    for c in range(len(cuts) - 1):
        for k in range(1, n_pair):
            block = direct(k, c)
            go(remote(block, block, f_send.at[k - 1, c], f_recv.at[k - 1, c], lab=core_peer))
    local[0].wait()
    local[1].wait()
    for k in range(n_z):
        block = group.at[1 - x, lax.rem(z + n_z - k, n_z)]
        remote(block, block, h_send.at[k], h_recv.at[k], blk=x_peer).wait_recv()

    def term(vectors, mask, block):
        margins = lax.dot_general(
            vectors, block, (((1,), (1,)), ((), ())), preferred_element_type=jnp.float32
        )
        return jnp.dot((mask * margins).astype(jnp.bfloat16), block, preferred_element_type=jnp.float32)

    def whole(at):
        return term(
            group[...].reshape(labels, depth), weights[at].reshape(labels, 2 * rows),
            slab[at].reshape(2 * rows, depth),
        ).reshape(acc.shape)

    def arrive(k):
        source = lax.rem(pair + n_pair - k, n_pair)
        direct(k, len(cuts) - 1)
        for c, piece in enumerate(cuts):
            block = slab.at[source, 1 - core, piece]
            remote(block, block, f_send.at[k - 1, c], f_recv.at[k - 1, c], lab=core_peer).wait_recv()
        return source

    other = slab.at[pair, 1 - core]
    remote(other, other, s_send.at[0], s_recv.at[0], lab=core_peer).wait_recv()
    acc[...] = whole(pair)
    if n_pair > 2:
        @pl.loop(1, n_pair - 1)
        def _(k):
            acc[...] += whole(arrive(k))

    last = arrive(n_pair - 1)

    def finish(half):
        acc[half] += term(
            group[half].reshape(labels // 2, depth), weights[last, half], slab[last].reshape(2 * rows, depth)
        ).reshape(acc.shape[1:])

    finish(1 - x)
    step = own // PIECES
    for i in range(n_z):
        to = lax.rem(z + 1 + i, n_z)
        for c in range(PIECES):
            piece = pl.ds(c * step, step)
            go(remote(
                acc.at[1 - x, to, piece], from_x.at[to, piece], x_send.at[i, c], x_recv.at[i, c], blk=x_peer
            ))
    finish(x)
    for i in range(n_z):
        to = lax.rem(z + 1 + i, n_z)
        for c in range(PIECES):
            piece = pl.ds(c * step, step)
            block = from_x.at[to, piece]
            remote(block, block, x_send.at[i, c], x_recv.at[i, c], blk=x_peer).wait_recv()
            acc[x, to, piece] += from_x[to, piece]
            if i < n_z - 1:
                go(remote(
                    acc.at[x, to, piece], from_z.at[i, piece], z_send.at[i, c], z_recv.at[i, c], blk=2 * to + x
                ))

    vectors = group[x, z].astype(jnp.float32)
    total = acc[x, z]
    for i in range(n_z - 1):
        for c in range(PIECES):
            block = from_z.at[i, pl.ds(c * step, step)]
            remote(block, block, z_send.at[i, c], z_recv.at[i, c], blk=x_peer).wait_recv()
        total += from_z[i]
    product = vectors + total
    hess[0] = product
    column = jnp.sum(vectors * product, axis=1, keepdims=True) / depth
    at_row = lax.broadcasted_iota(jnp.int32, (own, own), 0)
    at_column = lax.broadcasted_iota(jnp.int32, (own, own), 1)
    curve[...] = jnp.sum(jnp.where(at_row == at_column, column, 0.0), axis=0, keepdims=True)

    for copy in sent:
        copy.wait_send()


def solution(mesh):
    n_blk, n_lab = mesh.shape["blk"], mesh.shape["lab"]

    def shards(features, direction, active, shortlist):
        rows, depth = features.shape
        own = direction.shape[1]
        n_z, n_pair = n_blk // 2, n_lab // 2
        labels = n_blk * own
        dma = pltpu.SemaphoreType.DMA
        others = max(n_pair - 1, 1)
        scratch = [
            pltpu.VMEM((n_pair, 2, rows, depth), features.dtype),
            pltpu.VMEM((2, n_z, own, depth), direction.dtype),
            pltpu.VMEM(active.shape, active.dtype),
            pltpu.VMEM(shortlist.shape[::-1], shortlist.dtype),
            pltpu.VMEM((n_pair, 2, labels // 2, 2 * rows), jnp.float32),
            pltpu.VMEM((2, n_z, own, depth), jnp.float32),
            pltpu.VMEM((n_z, own, depth), jnp.float32),
            pltpu.VMEM((n_z - 1, own, depth), jnp.float32),
            dma((4,)),
            dma((others, 2)), dma((others, 2)),
            dma((1,)), dma((1,)),
            dma((others, 2)), dma((others, 2)),
            dma((n_z - 1,)), dma((n_z - 1,)),
            dma((n_z,)), dma((n_z,)),
            dma((n_z, PIECES)), dma((n_z, PIECES)),
            dma((n_z - 1, PIECES)), dma((n_z - 1, PIECES)),
        ]
        hbm = pl.BlockSpec(memory_space=pltpu.HBM)
        vmem = pl.BlockSpec(memory_space=pltpu.VMEM)
        return pl.pallas_call(
            functools.partial(kernel, n_blk, n_lab),
            out_shape=(
                pltpu.VMEM((1, own, depth), jnp.float32),
                pltpu.VMEM((1, own), jnp.float32),
            ),
            in_specs=[hbm, hbm, hbm, hbm],
            out_specs=(vmem, vmem),
            scratch_shapes=scratch,
            compiler_params=pltpu.CompilerParams(
                collective_id=0, has_side_effects=True, vmem_limit_bytes=60 << 20
            ),
            name="hessian",
        )(features, direction, active, shortlist.T)

    return jax.shard_map(
        shards,
        mesh=mesh,
        in_specs=(P(("blk", "lab"), None), P("lab", "blk", None), P("blk", "lab"), P("blk", "lab")),
        out_specs=(P("lab", "blk", None), P("lab", "blk")),
        check_vma=False,
    )
```

```python
import functools

import jax
import jax.numpy as jnp
from jax import lax
from jax.experimental import pallas as pl
from jax.experimental.pallas import tpu as pltpu
from jax.sharding import PartitionSpec as P

MESH = pl.DeviceIdType.MESH
TAIL = 16
PIECES = 2
STRAIGHT = 128


def remote(src, dst, send, recv, **where):
    return pltpu.make_async_remote_copy(
        src_ref=src, dst_ref=dst, send_sem=send, recv_sem=recv, device_id=where, device_id_type=MESH
    )


def kernel(
    n_blk, n_lab, feats, dirs, active, short, hess, curve,
    slab, group, act, tiles, weights, acc, from_x, from_z, from_far,
    local_sem, y_send, y_recv, s_send, s_recv, f_send, f_recv,
    g_send, g_recv, h_send, h_recv, x_send, x_recv, z_send, z_recv,
    d_send, d_recv,
):
    rows, depth = feats.shape
    own = dirs.shape[1]
    n_z, n_pair = n_blk // 2, n_lab // 2
    labels = n_blk * own
    cuts = (pl.ds(0, rows - TAIL), pl.ds(rows - TAIL, TAIL))
    blk, lab = lax.axis_index("blk"), lax.axis_index("lab")
    x, z = lax.rem(blk, 2), lax.div(blk, 2)
    core, pair = lax.rem(lab, 2), lax.div(lab, 2)
    x_peer = blk + 1 - 2 * x
    core_peer = lab + 1 - 2 * core

    local = [
        pltpu.make_async_copy(feats, slab.at[pair, core], local_sem.at[0]),
        pltpu.make_async_copy(dirs.at[0], group.at[x, z], local_sem.at[1]),
        pltpu.make_async_copy(active, act, local_sem.at[2]),
        pltpu.make_async_copy(short, tiles, local_sem.at[3]),
    ]
    barrier = pltpu.get_barrier_semaphore()
    for k in range(1, n_blk):
        pl.semaphore_signal(barrier, inc=1, device_id={"blk": lax.rem(blk + k, n_blk)}, device_id_type=MESH)
    for k in range(1, n_pair):
        for side in range(2):
            pl.semaphore_signal(
                barrier, inc=1, device_id={"lab": 2 * lax.rem(pair + k, n_pair) + side}, device_id_type=MESH
            )
    pl.semaphore_signal(barrier, inc=1, device_id={"lab": core_peer}, device_id_type=MESH)
    for copy in local:
        copy.start()
    pl.semaphore_wait(barrier, n_blk - 1 + 2 * n_pair - 1)

    sent = []

    def go(copy):
        copy.start()
        sent.append(copy)

    for k in range(1, n_z):
        go(remote(
            dirs.at[0], group.at[x, z], g_send.at[k - 1], g_recv.at[k - 1], blk=2 * lax.rem(z + k, n_z) + x
        ))
    go(remote(dirs.at[0], group.at[x, z], h_send.at[0], h_recv.at[0], blk=x_peer))
    for c, piece in enumerate(cuts):
        for k in range(1, n_pair):
            to = 2 * lax.rem(pair + k, n_pair)
            go(remote(
                feats.at[piece], slab.at[pair, core, piece], y_send.at[k - 1, c], y_recv.at[k - 1, c],
                lab=to + core,
            ))
            if c == len(cuts) - 1:
                go(remote(
                    feats.at[piece], slab.at[pair, core, piece], f_send.at[k - 1, c], f_recv.at[k - 1, c],
                    lab=to + 1 - core,
                ))
    go(remote(feats, slab.at[pair, core], s_send.at[0], s_recv.at[0], lab=core_peer))

    local[2].wait()
    local[3].wait()
    row_tile = active.shape[0] // short.shape[1]
    label_tile = active.shape[1] // short.shape[0]
    for r in range(short.shape[1]):
        for t in range(short.shape[0]):
            tile = act[r * row_tile:(r + 1) * row_tile, t * label_tile:(t + 1) * label_tile] * tiles[t:t + 1, r:r + 1]
            tile = tile.astype(jnp.float32).T
            at_pair, offset = divmod(r * row_tile, 2 * rows)
            for j in range(label_tile // own):
                device = t * (label_tile // own) + j
                slot = (device // 2) * own
                weights[at_pair, device % 2, slot:slot + own, offset:offset + row_tile] = tile[j * own:(j + 1) * own]

    for k in range(1, n_z):
        block = group.at[x, lax.rem(z + n_z - k, n_z)]
        remote(block, block, g_send.at[k - 1], g_recv.at[k - 1], blk=x_peer).wait_recv()
        go(remote(block, block, h_send.at[k], h_recv.at[k], blk=x_peer))

    def direct(k, c):
        block = slab.at[lax.rem(pair + n_pair - k, n_pair), core, cuts[c]]
        remote(block, block, y_send.at[k - 1, c], y_recv.at[k - 1, c], lab=core_peer).wait_recv()
        return block

    for c in range(len(cuts) - 1):
        for k in range(1, n_pair):
            block = direct(k, c)
            go(remote(block, block, f_send.at[k - 1, c], f_recv.at[k - 1, c], lab=core_peer))
    local[0].wait()
    local[1].wait()
    for k in range(n_z):
        block = group.at[1 - x, lax.rem(z + n_z - k, n_z)]
        remote(block, block, h_send.at[k], h_recv.at[k], blk=x_peer).wait_recv()

    def term(vectors, mask, block):
        margins = lax.dot_general(
            vectors, block, (((1,), (1,)), ((), ())), preferred_element_type=jnp.float32
        )
        return jnp.dot((mask * margins).astype(jnp.bfloat16), block, preferred_element_type=jnp.float32)

    def whole(at):
        return term(
            group[...].reshape(labels, depth), weights[at].reshape(labels, 2 * rows),
            slab[at].reshape(2 * rows, depth),
        ).reshape(acc.shape)

    def arrive(k):
        source = lax.rem(pair + n_pair - k, n_pair)
        direct(k, len(cuts) - 1)
        for c, piece in enumerate(cuts):
            block = slab.at[source, 1 - core, piece]
            remote(block, block, f_send.at[k - 1, c], f_recv.at[k - 1, c], lab=core_peer).wait_recv()
        return source

    other = slab.at[pair, 1 - core]
    remote(other, other, s_send.at[0], s_recv.at[0], lab=core_peer).wait_recv()
    acc[...] = whole(pair)
    if n_pair > 2:
        @pl.loop(1, n_pair - 1)
        def _(k):
            acc[...] += whole(arrive(k))

    last = arrive(n_pair - 1)

    def finish(half):
        acc[half] += term(
            group[half].reshape(labels // 2, depth), weights[last, half], slab[last].reshape(2 * rows, depth)
        ).reshape(acc.shape[1:])

    step = own // PIECES
    wide = pl.ds(STRAIGHT, depth - STRAIGHT)
    narrow = pl.ds(0, STRAIGHT)

    def straight(half, at):
        for i in range(n_z - 1):
            to = lax.rem(z + 1 + i, n_z)
            go(remote(
                acc.at[half, to, :, narrow], from_far.at[i, x], d_send.at[i, at], d_recv.at[i, x],
                blk=2 * to + half,
            ))

    def pieces(i):
        for c in range(PIECES):
            yield c, (pl.ds(c * step, step), wide if i < n_z - 1 else pl.ds(0, depth))

    finish(1 - x)
    for i in range(n_z):
        to = lax.rem(z + 1 + i, n_z)
        for c, piece in pieces(i):
            go(remote(
                acc.at[(1 - x, to, *piece)], from_x.at[(to, *piece)], x_send.at[i, c], x_recv.at[i, c], blk=x_peer
            ))
        if i == 0:
            straight(1 - x, 1)
    finish(x)
    straight(x, 0)
    for i in range(n_z):
        to = lax.rem(z + 1 + i, n_z)
        for c, piece in pieces(i):
            block = from_x.at[(to, *piece)]
            remote(block, block, x_send.at[i, c], x_recv.at[i, c], blk=x_peer).wait_recv()
            acc[(x, to, *piece)] += from_x[(to, *piece)]
            if i < n_z - 1:
                go(remote(
                    acc.at[(x, to, *piece)], from_z.at[(i, *piece)], z_send.at[i, c], z_recv.at[i, c],
                    blk=2 * to + x,
                ))

    vectors = group[x, z].astype(jnp.float32)
    for i in range(n_z - 1):
        for side in range(2):
            block = from_far.at[i, side]
            remote(block, block, d_send.at[i, side], d_recv.at[i, side], blk=x_peer).wait_recv()
        acc[x, z, :, narrow] += from_far[i, 0] + from_far[i, 1]
    for i in range(n_z - 1):
        for c, piece in pieces(i):
            block = from_z.at[(i, *piece)]
            remote(block, block, z_send.at[i, c], z_recv.at[i, c], blk=x_peer).wait_recv()
        acc[x, z, :, wide] += from_z[i, :, wide]
    total = acc[x, z]
    product = vectors + total
    hess[0] = product
    column = jnp.sum(vectors * product, axis=1, keepdims=True) / depth
    at_row = lax.broadcasted_iota(jnp.int32, (own, own), 0)
    at_column = lax.broadcasted_iota(jnp.int32, (own, own), 1)
    curve[...] = jnp.sum(jnp.where(at_row == at_column, column, 0.0), axis=0, keepdims=True)

    for copy in sent:
        copy.wait_send()


def solution(mesh):
    n_blk, n_lab = mesh.shape["blk"], mesh.shape["lab"]

    def shards(features, direction, active, shortlist):
        rows, depth = features.shape
        own = direction.shape[1]
        n_z, n_pair = n_blk // 2, n_lab // 2
        labels = n_blk * own
        dma = pltpu.SemaphoreType.DMA
        others = max(n_pair - 1, 1)
        scratch = [
            pltpu.VMEM((n_pair, 2, rows, depth), features.dtype),
            pltpu.VMEM((2, n_z, own, depth), direction.dtype),
            pltpu.VMEM(active.shape, active.dtype),
            pltpu.VMEM(shortlist.shape[::-1], shortlist.dtype),
            pltpu.VMEM((n_pair, 2, labels // 2, 2 * rows), jnp.float32),
            pltpu.VMEM((2, n_z, own, depth), jnp.float32),
            pltpu.VMEM((n_z, own, depth), jnp.float32),
            pltpu.VMEM((n_z - 1, own, depth), jnp.float32),
            pltpu.VMEM((n_z - 1, 2, own, STRAIGHT), jnp.float32),
            dma((4,)),
            dma((others, 2)), dma((others, 2)),
            dma((1,)), dma((1,)),
            dma((others, 2)), dma((others, 2)),
            dma((n_z - 1,)), dma((n_z - 1,)),
            dma((n_z,)), dma((n_z,)),
            dma((n_z, PIECES)), dma((n_z, PIECES)),
            dma((n_z - 1, PIECES)), dma((n_z - 1, PIECES)),
            dma((n_z - 1, 2)), dma((n_z - 1, 2)),
        ]
        hbm = pl.BlockSpec(memory_space=pltpu.HBM)
        vmem = pl.BlockSpec(memory_space=pltpu.VMEM)
        return pl.pallas_call(
            functools.partial(kernel, n_blk, n_lab),
            out_shape=(
                pltpu.VMEM((1, own, depth), jnp.float32),
                pltpu.VMEM((1, own), jnp.float32),
            ),
            in_specs=[hbm, hbm, hbm, hbm],
            out_specs=(vmem, vmem),
            scratch_shapes=scratch,
            compiler_params=pltpu.CompilerParams(
                collective_id=0, has_side_effects=True, vmem_limit_bytes=60 << 20
            ),
            name="hessian",
        )(features, direction, active, shortlist.T)

    return jax.shard_map(
        shards,
        mesh=mesh,
        in_specs=(P(("blk", "lab"), None), P("lab", "blk", None), P("blk", "lab"), P("blk", "lab")),
        out_specs=(P("lab", "blk", None), P("lab", "blk")),
        check_vma=False,
    )
```

```python
import functools

import jax
import jax.numpy as jnp
from jax import lax
from jax.experimental import pallas as pl
from jax.experimental.pallas import tpu as pltpu
from jax.sharding import PartitionSpec as P

MESH = pl.DeviceIdType.MESH
TAIL = 16
PIECES = 2


def remote(src, dst, send, recv, **where):
    return pltpu.make_async_remote_copy(
        src_ref=src, dst_ref=dst, send_sem=send, recv_sem=recv, device_id=where, device_id_type=MESH
    )


def kernel(
    n_blk, n_lab, feats, dirs, active, short, hess, curve,
    slab, group, act, tiles, weights, acc, from_x, from_z,
    local_sem, y_send, y_recv, s_send, s_recv, f_send, f_recv,
    g_send, g_recv, h_send, h_recv, x_send, x_recv, z_send, z_recv,
):
    rows, depth = feats.shape
    own = dirs.shape[1]
    n_z, n_pair = n_blk // 2, n_lab // 2
    labels = n_blk * own
    cuts = (pl.ds(0, rows - TAIL), pl.ds(rows - TAIL, TAIL))
    blk, lab = lax.axis_index("blk"), lax.axis_index("lab")
    x, z = lax.rem(blk, 2), lax.div(blk, 2)
    core, pair = lax.rem(lab, 2), lax.div(lab, 2)
    x_peer = blk + 1 - 2 * x
    core_peer = lab + 1 - 2 * core

    local = [
        pltpu.make_async_copy(feats, slab.at[pair, core], local_sem.at[0]),
        pltpu.make_async_copy(dirs.at[0], group.at[x, z], local_sem.at[1]),
        pltpu.make_async_copy(active, act, local_sem.at[2]),
        pltpu.make_async_copy(short, tiles, local_sem.at[3]),
    ]
    barrier = pltpu.get_barrier_semaphore()
    for k in range(1, n_z):
        pl.semaphore_signal(
            barrier, inc=1, device_id={"blk": 2 * lax.rem(z + k, n_z) + x}, device_id_type=MESH
        )
    pl.semaphore_signal(barrier, inc=1, device_id={"blk": x_peer}, device_id_type=MESH)
    for k in range(1, n_pair):
        for side in range(2):
            pl.semaphore_signal(
                barrier, inc=1, device_id={"lab": 2 * lax.rem(pair + k, n_pair) + side}, device_id_type=MESH
            )
    pl.semaphore_signal(barrier, inc=1, device_id={"lab": core_peer}, device_id_type=MESH)
    for copy in local:
        copy.start()
    pl.semaphore_wait(barrier, n_z + 2 * n_pair - 1)

    sent = []

    def go(copy):
        copy.start()
        sent.append(copy)

    for k in range(1, n_z):
        go(remote(
            dirs.at[0], group.at[x, z], g_send.at[k - 1], g_recv.at[k - 1], blk=2 * lax.rem(z + k, n_z) + x
        ))
    go(remote(dirs.at[0], group.at[x, z], h_send.at[0], h_recv.at[0], blk=x_peer))
    for c, piece in enumerate(cuts):
        for k in range(1, n_pair):
            to = 2 * lax.rem(pair + k, n_pair)
            go(remote(
                feats.at[piece], slab.at[pair, core, piece], y_send.at[k - 1, c], y_recv.at[k - 1, c],
                lab=to + core,
            ))
            if c == len(cuts) - 1:
                go(remote(
                    feats.at[piece], slab.at[pair, core, piece], f_send.at[k - 1, c], f_recv.at[k - 1, c],
                    lab=to + 1 - core,
                ))
    go(remote(feats, slab.at[pair, core], s_send.at[0], s_recv.at[0], lab=core_peer))

    local[2].wait()
    local[3].wait()
    row_tile = active.shape[0] // short.shape[1]
    label_tile = active.shape[1] // short.shape[0]
    for r in range(short.shape[1]):
        for t in range(short.shape[0]):
            tile = act[r * row_tile:(r + 1) * row_tile, t * label_tile:(t + 1) * label_tile] * tiles[t:t + 1, r:r + 1]
            tile = tile.astype(jnp.float32).T
            at_pair, offset = divmod(r * row_tile, 2 * rows)
            for j in range(label_tile // own):
                device = t * (label_tile // own) + j
                slot = (device // 2) * own
                weights[at_pair, device % 2, slot:slot + own, offset:offset + row_tile] = tile[j * own:(j + 1) * own]

    for k in range(1, n_z):
        block = group.at[x, lax.rem(z + n_z - k, n_z)]
        remote(block, block, g_send.at[k - 1], g_recv.at[k - 1], blk=x_peer).wait_recv()
        go(remote(block, block, h_send.at[k], h_recv.at[k], blk=x_peer))

    def direct(k, c):
        block = slab.at[lax.rem(pair + n_pair - k, n_pair), core, cuts[c]]
        remote(block, block, y_send.at[k - 1, c], y_recv.at[k - 1, c], lab=core_peer).wait_recv()
        return block

    for c in range(len(cuts) - 1):
        for k in range(1, n_pair):
            block = direct(k, c)
            go(remote(block, block, f_send.at[k - 1, c], f_recv.at[k - 1, c], lab=core_peer))
    local[0].wait()
    local[1].wait()
    for k in range(n_z):
        block = group.at[1 - x, lax.rem(z + n_z - k, n_z)]
        remote(block, block, h_send.at[k], h_recv.at[k], blk=x_peer).wait_recv()

    def term(vectors, mask, block):
        margins = lax.dot_general(
            vectors, block, (((1,), (1,)), ((), ())), preferred_element_type=jnp.float32
        )
        return jnp.dot((mask * margins).astype(jnp.bfloat16), block, preferred_element_type=jnp.float32)

    def whole(at):
        return term(
            group[...].reshape(labels, depth), weights[at].reshape(labels, 2 * rows),
            slab[at].reshape(2 * rows, depth),
        ).reshape(acc.shape)

    def arrive(k):
        source = lax.rem(pair + n_pair - k, n_pair)
        direct(k, len(cuts) - 1)
        for c, piece in enumerate(cuts):
            block = slab.at[source, 1 - core, piece]
            remote(block, block, f_send.at[k - 1, c], f_recv.at[k - 1, c], lab=core_peer).wait_recv()
        return source

    other = slab.at[pair, 1 - core]
    remote(other, other, s_send.at[0], s_recv.at[0], lab=core_peer).wait_recv()
    acc[...] = whole(pair)
    if n_pair > 2:
        @pl.loop(1, n_pair - 1)
        def _(k):
            acc[...] += whole(arrive(k))

    last = arrive(n_pair - 1)

    def finish(half):
        acc[half] += term(
            group[half].reshape(labels // 2, depth), weights[last, half], slab[last].reshape(2 * rows, depth)
        ).reshape(acc.shape[1:])

    def partner(i):
        to, bit = z, 1
        while bit < n_z:
            if (n_z - 1 - i) & bit:
                to = to + bit * (1 - 2 * lax.rem(lax.div(z, bit), 2))
            bit *= 2
        return to

    finish(1 - x)
    step = own // PIECES
    for i in range(n_z):
        to = partner(i)
        for c in range(PIECES):
            piece = pl.ds(c * step, step)
            go(remote(
                acc.at[1 - x, to, piece], from_x.at[to, piece], x_send.at[i, c], x_recv.at[i, c], blk=x_peer
            ))
    finish(x)
    for i in range(n_z):
        to = partner(i)
        for c in range(PIECES):
            piece = pl.ds(c * step, step)
            block = from_x.at[to, piece]
            remote(block, block, x_send.at[i, c], x_recv.at[i, c], blk=x_peer).wait_recv()
            acc[x, to, piece] += from_x[to, piece]
            if i < n_z - 1:
                go(remote(
                    acc.at[x, to, piece], from_z.at[i, piece], z_send.at[i, c], z_recv.at[i, c], blk=2 * to + x
                ))

    vectors = group[x, z].astype(jnp.float32)
    total = acc[x, z]
    for i in range(n_z - 1):
        for c in range(PIECES):
            block = from_z.at[i, pl.ds(c * step, step)]
            remote(block, block, z_send.at[i, c], z_recv.at[i, c], blk=x_peer).wait_recv()
        total += from_z[i]
    product = vectors + total
    hess[0] = product
    column = jnp.sum(vectors * product, axis=1, keepdims=True) / depth
    at_row = lax.broadcasted_iota(jnp.int32, (own, own), 0)
    at_column = lax.broadcasted_iota(jnp.int32, (own, own), 1)
    curve[...] = jnp.sum(jnp.where(at_row == at_column, column, 0.0), axis=0, keepdims=True)

    for copy in sent:
        copy.wait_send()


def solution(mesh):
    n_blk, n_lab = mesh.shape["blk"], mesh.shape["lab"]

    def shards(features, direction, active, shortlist):
        rows, depth = features.shape
        own = direction.shape[1]
        n_z, n_pair = n_blk // 2, n_lab // 2
        labels = n_blk * own
        dma = pltpu.SemaphoreType.DMA
        others = max(n_pair - 1, 1)
        scratch = [
            pltpu.VMEM((n_pair, 2, rows, depth), features.dtype),
            pltpu.VMEM((2, n_z, own, depth), direction.dtype),
            pltpu.VMEM(active.shape, active.dtype),
            pltpu.VMEM(shortlist.shape[::-1], shortlist.dtype),
            pltpu.VMEM((n_pair, 2, labels // 2, 2 * rows), jnp.float32),
            pltpu.VMEM((2, n_z, own, depth), jnp.float32),
            pltpu.VMEM((n_z, own, depth), jnp.float32),
            pltpu.VMEM((n_z - 1, own, depth), jnp.float32),
            dma((4,)),
            dma((others, 2)), dma((others, 2)),
            dma((1,)), dma((1,)),
            dma((others, 2)), dma((others, 2)),
            dma((n_z - 1,)), dma((n_z - 1,)),
            dma((n_z,)), dma((n_z,)),
            dma((n_z, PIECES)), dma((n_z, PIECES)),
            dma((n_z - 1, PIECES)), dma((n_z - 1, PIECES)),
        ]
        hbm = pl.BlockSpec(memory_space=pltpu.HBM)
        vmem = pl.BlockSpec(memory_space=pltpu.VMEM)
        return pl.pallas_call(
            functools.partial(kernel, n_blk, n_lab),
            out_shape=(
                pltpu.VMEM((1, own, depth), jnp.float32),
                pltpu.VMEM((1, own), jnp.float32),
            ),
            in_specs=[hbm, hbm, hbm, hbm],
            out_specs=(vmem, vmem),
            scratch_shapes=scratch,
            compiler_params=pltpu.CompilerParams(
                collective_id=0, has_side_effects=True, vmem_limit_bytes=60 << 20
            ),
            name="hessian",
        )(features, direction, active, shortlist.T)

    return jax.shard_map(
        shards,
        mesh=mesh,
        in_specs=(P(("blk", "lab"), None), P("lab", "blk", None), P("blk", "lab"), P("blk", "lab")),
        out_specs=(P("lab", "blk", None), P("lab", "blk")),
        check_vma=False,
    )
```
